256 devices in a mesh: tile: 32 (over y, x, z_lo), seq: 8 (over z_hi, core).
Axes of the slice: x: 4, y: 4, z: 8 (z_hi: 4, z_lo: 2; z = z_hi * 2 + z_lo), core: 2. Of those that a mesh axis runs over, the one named last changes fastest.
Arguments:
- latent_rows: bfloat16 [512, 2, 16, 5120], P(('tile', 'seq')), may hold values from -400 to 400
- col_weight: int32 [32, 16], replicated, may hold values from 1 to 16
- row_weight: int32 [32, 16], replicated, may hold values from 1 to 16
- shift_mod: float32 [5120], replicated, may hold values from -3 to 3
- scale_mod: float32 [5120], replicated, may hold values from -3 to 3
- w_query: bfloat16 [5120, 3072], P(None, 'seq'), may hold values from -0.15625 to 0.15625
- w_key: bfloat16 [5120, 3072], P(None, 'seq'), may hold values from -0.078125 to 0.078125
- w_value: bfloat16 [5120, 3072], P(None, 'seq'), may hold values from -0.078125 to 0.078125
Outputs:
- attention: bfloat16 [16384, 3072], P('tile', 'seq')
The draws below stay inside these ranges and needn't reach their ends.
All inputs are finite; a program needn't handle non-finite values.
Results may differ from the reference program's by a relative error of at most 0.013.
Values may be sent and summed in bfloat16 or wider, within the bound.
No kernel may reach another device: no remote copies, remote signals or barrier semaphores. Data moves between devices by JAX's collectives and lax.ppermute only.
A program may use at most 128 MiB of HBM per device.

```python
import math
from functools import partial
import jax
import jax.numpy as jnp
from jax import lax

D = 5120
HEADS = 24
HD = 128
GC = 4
TW = 16
FR = 2
OV = 8
OH = 2
TILES = 32
TH = 16


def draw_latent_rows(key, part):
    key = jax.random.fold_in(key, 11)
    key_base, key_row, key_col = jax.random.split(key, 3)
    shape_all = (TILES * TH, FR, TW, D)
    base_vals = jnp.clip(jax.random.normal(key_base, shape_all, jnp.float32), -4.0, 4.0)
    row_scale = jnp.exp(jax.random.uniform(key_row, (TILES * TH, FR, TW, 1), jnp.float32, 0.0, math.log(10.0)))
    col_scale = jnp.exp(jax.random.uniform(key_col, (D,), jnp.float32, 0.0, math.log(10.0)))
    return (base_vals * row_scale * col_scale).astype(jnp.bfloat16)


def with_ends(drawn, rng, least, largest):
    extent = drawn.shape
    spot = [jax.random.randint(jax.random.fold_in(rng, axis), (), 0, extent[axis]) for axis in range(len(extent))]
    drawn = drawn.at[tuple(spot)].set(least)
    longest = extent.index(max(extent))
    spot[longest] = (spot[longest] + 1) % extent[longest]
    return drawn.at[tuple(spot)].set(largest)


def shard_levels(stream_key, dims, cuts, least, top_value):
    def one(dim, blocks):
        heights = jax.random.uniform(jax.random.fold_in(jax.random.fold_in(stream_key, 6), dim), (blocks,), jnp.float32, least / len(cuts), top_value / len(cuts))
        return jnp.repeat(jnp.exp(heights), dims[dim] // blocks).reshape((-1,) + (1,) * (len(dims) - dim - 1))

    level = one(*cuts[0])
    for cut in cuts[1:]:
        level = level * one(*cut)
    return level


def normal_values(own_key, shape, scale, most, cuts=(), kind=jnp.bfloat16):
    factor_of = shard_levels(own_key, shape, cuts, -0.22, 0.18) if cuts else 1.0
    entries = jax.random.normal(own_key, shape, jnp.float32) * scale * factor_of
    return jnp.minimum(jnp.maximum(entries, -most), most).astype(kind)


def setup_inputs(seed: int = 0) -> dict:
    arg_keys = jax.random.split(jax.random.key(seed), 9)
    return {
        "latent_rows": draw_latent_rows(jax.random.fold_in(arg_keys[8], 71), 0),
        "col_weight": with_ends(jax.random.randint(arg_keys[1], (TILES, TW), 1, 17), jax.random.fold_in(arg_keys[1], 1), 1, 16).astype(jnp.int32),
        "row_weight": with_ends(jax.random.randint(arg_keys[2], (TILES, TH), 1, 17), jax.random.fold_in(arg_keys[2], 1), 1, 16).astype(jnp.int32),
        "shift_mod": normal_values(arg_keys[3], (D,), 0.5, 3.0, (), jnp.float32),
        "scale_mod": normal_values(arg_keys[4], (D,), 0.5, 3.0, (), jnp.float32),
        "w_query": normal_values(arg_keys[5], (D, HEADS * HD), (D // 4) ** -0.5, 0.15625, ((1, 8),)),
        "w_key": normal_values(arg_keys[6], (D, HEADS * HD), D ** -0.5, 0.078125, ((1, 8),)),
        "w_value": normal_values(arg_keys[7], (D, HEADS * HD), D ** -0.5, 0.078125, ((1, 8),)),
    }


def blend_with(own_vals, own_w, head_vals, head_w, tail_vals, tail_w, along):
    full_len = own_vals.shape[along]
    head_len = head_vals.shape[along]
    tail_len = tail_vals.shape[along]
    pad_head = [(0, 0)] * own_vals.ndim
    pad_head[along] = (0, full_len - head_len)
    pad_tail = [(0, 0)] * own_vals.ndim
    pad_tail[along] = (full_len - tail_len, 0)
    heads_full = jnp.pad(head_vals.astype(jnp.float32), pad_head)
    tails_full = jnp.pad(tail_vals.astype(jnp.float32), pad_tail)
    head_wfull = jnp.pad(head_w, (0, full_len - head_len))
    tail_wfull = jnp.pad(tail_w, (full_len - tail_len, 0))
    shape_w = [1] * own_vals.ndim
    shape_w[along] = full_len
    numer = own_vals.astype(jnp.float32) * own_w.reshape(shape_w) + heads_full * head_wfull.reshape(shape_w) + tails_full * tail_wfull.reshape(shape_w)
    return numer / (own_w + head_wfull + tail_wfull).reshape(shape_w)

def modulate(blended, shift_mod, scale_mod):
    floats = blended.astype(jnp.float32)
    row_mean = lax.optimization_barrier(jnp.mean(floats, axis=-1, keepdims=True))
    centred = floats - row_mean
    row_var = lax.optimization_barrier(jnp.mean(centred * centred, axis=-1, keepdims=True))
    return (centred * lax.rsqrt(row_var + 1e-06) * (1.0 + scale_mod) + shift_mod).astype(jnp.bfloat16)

def attend(token_rows, w_query, w_key, w_value):
    row_count = token_rows.shape[0]
    queries = jnp.dot(token_rows, w_query, preferred_element_type=jnp.float32).astype(jnp.bfloat16).reshape(row_count, HEADS, HD)
    key_rows = jnp.dot(token_rows, w_key, preferred_element_type=jnp.float32).astype(jnp.bfloat16).reshape(row_count, HEADS, HD)
    values = jnp.dot(token_rows, w_value, preferred_element_type=jnp.float32).astype(jnp.bfloat16).reshape(row_count, HEADS, HD)
    scores = jnp.einsum('qhd,khd->hqk', queries.astype(jnp.float32), key_rows.astype(jnp.float32)) * HD ** (-0.5)
    raised = jnp.exp(scores)
    weights_bf = (raised / lax.optimization_barrier(jnp.sum(raised, axis=-1, keepdims=True))).astype(jnp.bfloat16)
    output = jnp.einsum('hqk,khd->qhd', weights_bf.astype(jnp.float32), values.astype(jnp.float32))
    return output.astype(jnp.bfloat16).reshape(row_count, HEADS * HD)

def reference(latent_rows, col_weight, row_weight, shift_mod, scale_mod, w_query, w_key, w_value):
    tile_grid = latent_rows.reshape(TILES, TH, FR, TW, D)
    places = jnp.arange(TILES, dtype=jnp.int32)
    grid_col = places % GC
    grid_row = places // GC
    west_on = (grid_col > 0).astype(jnp.float32)
    east_on = (grid_col < GC - 1).astype(jnp.float32)
    north_on = (grid_row > 0).astype(jnp.float32)
    south_on = (grid_row < TILES // GC - 1).astype(jnp.float32)
    col_all = col_weight.astype(jnp.float32)
    row_all = row_weight.astype(jnp.float32)
    west_w = jnp.roll(col_all, 1, 0)[:, TW - OV:] * west_on[:, None]
    east_w = jnp.roll(col_all, -1, 0)[:, :OV] * east_on[:, None]
    west_vals = jnp.roll(tile_grid, 1, 0)[:, :, :, TW - OV:]
    east_vals = jnp.roll(tile_grid, -1, 0)[:, :, :, :OV]
    col_mixed = jax.vmap(partial(blend_with, along=2))(tile_grid, col_all, west_vals, west_w, east_vals, east_w).astype(jnp.bfloat16)
    north_w = jnp.roll(row_all, GC, 0)[:, TH - OH:] * north_on[:, None]
    south_w = jnp.roll(row_all, -GC, 0)[:, :OH] * south_on[:, None]
    north_vals = jnp.roll(col_mixed, GC, 0)[:, TH - OH:]
    south_vals = jnp.roll(col_mixed, -GC, 0)[:, :OH]
    blended = jax.vmap(partial(blend_with, along=0))(col_mixed, row_all, north_vals, north_w, south_vals, south_w).astype(jnp.bfloat16)
    normed = modulate(blended, shift_mod, scale_mod).reshape(TILES, TH * FR * TW, D)
    outputs = lax.map(lambda token_rows: attend(token_rows, w_query, w_key, w_value), normed)
    return outputs.reshape(TILES * TH * FR * TW, HEADS * HD)
```

```python
import jax
import jax.numpy as jnp
from jax import lax
from jax.sharding import Mesh, PartitionSpec as P

HD = 128
GC = 4
OV = 8
OH = 2
AX = ("y", "x", "zl", "zh", "c")


def ring(n, by):
    return [(i, (i + by) % n) for i in range(n)]


SWAP = [(0, 1), (1, 0)]
OUTER_PAIRS = [(1, 2), (2, 1), (5, 6), (6, 5)]


def row_pairs():
    pairs = []
    for t in range(28):
        pairs.append((t * 8 + 7, (t + 4) * 8))
        pairs.append(((t + 4) * 8, t * 8 + 7))
    return pairs


def take_row(table, index):
    return lax.dynamic_index_in_dim(table, index, 0, keepdims=False)


def modulate(blended, shift_mod, scale_mod):
    floats = blended.astype(jnp.float32)
    row_mean = jnp.mean(floats, axis=-1, keepdims=True)
    centred = floats - row_mean
    row_var = jnp.mean(centred * centred, axis=-1, keepdims=True)
    return (centred * lax.rsqrt(row_var + 1e-06) * (1.0 + scale_mod) + shift_mod).astype(
        jnp.bfloat16
    )


def local(latent_rows, col_weight, row_weight, shift_mod, scale_mod, w_query, w_key, w_value):
    y, x, zl, zh, c = (lax.axis_index(a) for a in AX)
    tile = y * 8 + x * 2 + zl
    seq = zh * 2 + c
    gcol = tile % GC
    low = zl == 0
    col_all = col_weight.astype(jnp.float32)
    row_all = row_weight.astype(jnp.float32)
    own_cols = take_row(col_all, tile)
    west = take_row(col_all, jnp.maximum(tile - 1, 0))
    east = take_row(col_all, jnp.minimum(tile + 1, 31))
    left, right = latent_rows[:, :, :OV], latent_rows[:, :, OV:]
    outer = jnp.where(low, left, right)
    inner = jnp.where(low, right, left)
    in_other = lax.ppermute(inner, "zl", SWAP)
    out_other = lax.ppermute(outer, ("x", "zl"), OUTER_PAIRS)
    in_w = jnp.where(low, own_cols[OV:], own_cols[:OV])
    in_wo = jnp.where(low, east[:OV], west[OV:])
    out_w = jnp.where(low, own_cols[:OV], own_cols[OV:])
    has_out = ((gcol == 1) | (gcol == 2)).astype(jnp.float32)
    out_wo = jnp.where(low, west[OV:], east[:OV]) * has_out

    def blend(a, wa, b, wb):
        numer = a.astype(jnp.float32) * wa + b.astype(jnp.float32) * wb
        return (numer / (wa + wb)).astype(jnp.bfloat16)

    outer = blend(outer, out_w[:, None], out_other, out_wo[:, None])
    inner = blend(inner, in_w[:, None], in_other, in_wo[:, None])
    both = jnp.stack([outer, inner], 0)
    other = lax.ppermute(both, AX, row_pairs())
    rw = take_row(row_all, tile)
    own_r = lax.dynamic_slice(rw, (2 * seq,), (2,))
    north = take_row(row_all, jnp.maximum(tile - GC, 0))[14:]
    south = take_row(row_all, jnp.minimum(tile + GC, 31))[:OH]
    on_n = ((seq == 0) & (tile >= GC)).astype(jnp.float32)
    on_s = ((seq == 7) & (tile < 28)).astype(jnp.float32)
    oth_r = jnp.where(seq == 0, north * on_n, south * on_s)
    both = blend(both, own_r[None, :, None, None, None], other, oth_r[None, :, None, None, None])
    normed = modulate(both, shift_mod, scale_mod)
    own = normed.reshape(64, -1)

    def weights_on(rows):
        return [
            jnp.dot(rows, w, preferred_element_type=jnp.float32).astype(jnp.bfloat16)
            for w in (w_query, w_key, w_value)
        ]

    def core_swap(v):
        return lax.ppermute(v, "c", SWAP)

    own_x = core_swap(own)
    from_prev = lax.ppermute(own, "zh", ring(4, 1))
    from_next = lax.ppermute(own, "zh", ring(4, -1))
    far_a = lax.ppermute(from_prev[:32], "zh", ring(4, 1))
    far_b = lax.ppermute(from_next[32:], "zh", ring(4, -1))
    mid = jnp.concatenate([from_prev, from_next], 0)
    mid_x = core_swap(mid)
    last = jnp.concatenate([far_a, far_b], 0)
    last_x = core_swap(last)
    parts = [weights_on(v) for v in (own, own_x, mid, mid_x, last, last_x)]

    def joined(k):
        a, ax, m, mx, l, lx = (p[k] for p in parts)
        m, mx = m.reshape(2, 64, -1), mx.reshape(2, 64, -1)
        mine = jnp.stack([a, m[0], m[1], l], 0)
        theirs = jnp.stack([ax, mx[0], mx[1], lx], 0)
        return jnp.stack([mine, theirs], 0).reshape(512, -1, HD)

    q, k, v = joined(0), joined(1), joined(2)
    scores = jnp.einsum("qhd,khd->hqk", q, k, preferred_element_type=jnp.float32) * HD ** (-0.5)
    raised = jnp.exp(scores)
    wts = (raised / jnp.sum(raised, axis=-1, keepdims=True)).astype(jnp.bfloat16)
    out = jnp.einsum("hqk,khd->qhd", wts, v, preferred_element_type=jnp.float32)
    out = out.astype(jnp.bfloat16).reshape(2, 4, 2, 4, 8, -1)
    order = jnp.stack([zh, (zh + 3) % 4, (zh + 1) % 4, (zh + 2) % 4])
    place = jnp.zeros((4,), jnp.int32).at[order].set(jnp.arange(4, dtype=jnp.int32))
    out = jnp.take(out, place, axis=1)
    out = jnp.where(c == 0, out, out[::-1])
    out = jnp.where(low, out, out[:, :, ::-1])
    return out.transpose(1, 0, 3, 2, 4, 5).reshape(512, -1)


def solution(mesh):
    fine = Mesh(mesh.devices.reshape(4, 4, 2, 4, 2), AX)
    in_specs = (
        P(AX, None, None, None),
        P(),
        P(),
        P(),
        P(),
        P(None, ("zh", "c")),
        P(None, ("zh", "c")),
        P(None, ("zh", "c")),
    )
    out_specs = P(("y", "x", "zl"), ("zh", "c"))
    return jax.shard_map(local, mesh=fine, in_specs=in_specs, out_specs=out_specs, check_vma=False)
```

```python
import jax
import jax.numpy as jnp
from jax import lax
from jax.experimental import pallas as pl
from jax.experimental.pallas import tpu as pltpu
from jax.sharding import Mesh, PartitionSpec as P

HD = 128
GC = 4
OV = 8
OH = 2
AX = ("y", "x", "zl", "zh", "c")
SLOTS = 4


OUTER_PAIRS = [(1, 2), (2, 1), (5, 6), (6, 5)]
SWAP = [(0, 1), (1, 0)]


def ring(by):
    return [(g, (g + by) % 4) for g in range(4)]


def row_pairs(neighbour):
    pairs = []
    for t in range(32 - GC):
        n = neighbour(t)
        if n is not None:
            pairs.append((n * 8 + 7, (t + GC) * 8))
            pairs.append(((n + GC) * 8, t * 8 + 7))
    return pairs


def itself(t):
    return t


def inner_of(t):
    return t ^ 1


def outer_of(t):
    return {0: None, 1: t + 1, 2: t - 1, 3: None}[t % GC]


def take_row(table, index):
    return lax.dynamic_index_in_dim(table, index, 0, keepdims=False)


def modulate(blended, shift_mod, scale_mod):
    floats = blended.astype(jnp.float32)
    row_mean = jnp.mean(floats, axis=-1, keepdims=True)
    centred = floats - row_mean
    row_var = jnp.mean(centred * centred, axis=-1, keepdims=True)
    return (centred * lax.rsqrt(row_var + 1e-06) * (1.0 + scale_mod) + shift_mod).astype(
        jnp.bfloat16
    )


def blend(a, wa, b, wb):
    numer = a.astype(jnp.float32) * wa + b.astype(jnp.float32) * wb
    return (numer / (wa + wb)).astype(jnp.bfloat16)


def local(latent_rows, col_weight, row_weight, shift_mod, scale_mod, w_query, w_key, w_value):
    y, x, zl, zh, c = (lax.axis_index(a) for a in AX)
    tile = y * 8 + x * 2 + zl
    gcol = tile % GC
    low = zl == 0
    top_here = (zh == 0) & (c == 0) & (tile >= GC)
    bottom_here = (zh == 3) & (c == 1) & (tile < 32 - GC)
    col_all = col_weight.astype(jnp.float32)
    row_all = row_weight.astype(jnp.float32)
    partner = jnp.where(zh == 0, jnp.maximum(tile - GC, 0), jnp.minimum(tile + GC, 31))
    left, right = latent_rows[:, :, :OV], latent_rows[:, :, OV:]
    outer = jnp.where(low, left, right)
    inner = jnp.where(low, right, left)

    def col_mix(t, v, out_other, in_other):
        own_cols = take_row(col_all, t)
        west = take_row(col_all, jnp.maximum(t - 1, 0))[OV:] * (gcol > 0)
        east = take_row(col_all, jnp.minimum(t + 1, 31))[:OV] * (gcol < GC - 1)
        other = jnp.concatenate(
            [jnp.where(low, out_other, in_other), jnp.where(low, in_other, out_other)], 2
        )
        return blend(v, own_cols[:, None], other, jnp.concatenate([west, east])[:, None])

    far_rows = lax.ppermute(latent_rows, AX, row_pairs(itself))
    far_outer = lax.ppermute(outer, AX, row_pairs(outer_of))
    far_inner = lax.ppermute(inner, AX, row_pairs(inner_of))
    out_other = lax.ppermute(outer, ("x", "zl"), OUTER_PAIRS)
    in_other = lax.ppermute(inner, "zl", SWAP)
    own = col_mix(tile, latent_rows, out_other, in_other)
    other = col_mix(partner, far_rows, far_outer, far_inner)
    own_r = lax.dynamic_slice(take_row(row_all, tile), (4 * zh + 2 * c,), (OH,))
    other_r = take_row(row_all, partner)
    other_r = jnp.where(zh == 0, other_r[14:], other_r[:OH]) * (top_here | bottom_here)
    own = blend(own, own_r[:, None, None, None], other, other_r[:, None, None, None])
    own = modulate(own, shift_mod, scale_mod).reshape(64, -1)

    def core_swap(v):
        return lax.ppermute(v, "c", SWAP)

    def weights_on(rows):
        return [
            jnp.dot(rows, w, preferred_element_type=jnp.float32).astype(jnp.bfloat16)
            for w in (w_query, w_key, w_value)
        ]

    def both_cores(v):
        return jnp.concatenate([v, core_swap(v)], 0)

    prev = lax.ppermute(own, "zh", ring(1))
    nxt = lax.ppermute(own, "zh", ring(-1))
    own_q = weights_on(both_cores(own))
    prev, nxt, *own_q = lax.optimization_barrier((prev, nxt, *own_q))
    side = jnp.concatenate([prev, nxt], 0)
    far = [lax.ppermute(side[:32], "zh", ring(1)), lax.ppermute(side[96:], "zh", ring(-1))]
    side_q, side_x = weights_on(side), weights_on(core_swap(side))
    *far, side_q, side_x = lax.optimization_barrier((*far, side_q, side_x))
    far = jnp.concatenate(far, 0)
    far_q = weights_on(both_cores(far))
    at = [
        (((zh - d) % 4) * 2 + core) * 64 for core in (c, 1 - c) for d in (0, 1, 3, 2)
    ]
    return attention(jnp.stack(at).astype(jnp.int32), own_q, side_q, side_x, far_q)


def attention_kernel(at, *refs):
    parts, (out, *wholes) = refs[:12], refs[12:]

    def put(whole, n, rows):
        whole[pl.ds(pl.multiple_of(at[n], 64), 64), :] = rows

    for n, whole in enumerate(wholes):
        own, side, side_x, far = parts[n::3]
        for core, pair in enumerate((side, side_x)):
            rows = slice(core * 64, core * 64 + 64)
            put(whole, core * 4, own[rows, :])
            put(whole, core * 4 + 1, pair[:64, :])
            put(whole, core * 4 + 2, pair[64:, :])
            put(whole, core * 4 + 3, far[rows, :])
    q_all, k_all, v_all = wholes
    for h in range(out.shape[1] // HD):
        cols = slice(h * HD, h * HD + HD)
        scores = lax.dot_general(
            q_all[:, cols],
            k_all[:, cols],
            (((1,), (1,)), ((), ())),
            preferred_element_type=jnp.float32,
        ) * HD ** (-0.5)
        raised = jnp.exp(scores)
        wts = (raised / jnp.sum(raised, axis=-1, keepdims=True)).astype(jnp.bfloat16)
        out[:, cols] = jnp.dot(
            wts, v_all[:, cols], preferred_element_type=jnp.float32
        ).astype(jnp.bfloat16)


def attention(at, *groups):
    width = groups[0][0].shape[1]
    here = pl.BlockSpec(memory_space=pltpu.VMEM)
    return pl.pallas_call(
        attention_kernel,
        out_shape=jax.ShapeDtypeStruct((512, width), jnp.bfloat16),
        in_specs=[pl.BlockSpec(memory_space=pltpu.SMEM)] + [here] * 12,
        out_specs=here,
        scratch_shapes=[pltpu.VMEM((512, width), jnp.bfloat16)] * 3,
        compiler_params=pltpu.CompilerParams(vmem_limit_bytes=12 * 1024 * 1024),
    )(at, *(v for g in groups for v in g))


def solution(mesh):
    fine = Mesh(mesh.devices.reshape(4, 4, 2, 4, 2), AX)
    in_specs = (
        P(AX, None, None, None),
        P(),
        P(),
        P(),
        P(),
        P(None, ("zh", "c")),
        P(None, ("zh", "c")),
        P(None, ("zh", "c")),
    )
    out_specs = P(("y", "x", "zl"), ("zh", "c"))
    return jax.shard_map(local, mesh=fine, in_specs=in_specs, out_specs=out_specs, check_vma=False)
```

```python
import jax
import jax.numpy as jnp
from jax import lax
from jax.experimental import pallas as pl
from jax.experimental.pallas import tpu as pltpu
from jax.sharding import Mesh, PartitionSpec as P

HD = 128
GC = 4
OV = 8
OH = 2
AX = ("y", "x", "zl", "zh", "c")
SLOTS = 4


OUTER_PAIRS = [(1, 2), (2, 1), (5, 6), (6, 5)]
SWAP = [(0, 1), (1, 0)]


def ring(by):
    return [(g, (g + by) % 4) for g in range(4)]


def row_pairs(neighbour):
    pairs = []
    for t in range(32 - GC):
        n = neighbour(t)
        if n is not None:
            pairs.append((n * 8 + 7, (t + GC) * 8))
            pairs.append(((n + GC) * 8, t * 8 + 7))
    return pairs


def itself(t):
    return t


def inner_of(t):
    return t ^ 1


def outer_of(t):
    return {0: None, 1: t + 1, 2: t - 1, 3: None}[t % GC]


def take_row(table, index):
    return lax.dynamic_index_in_dim(table, index, 0, keepdims=False)


def modulate(blended, shift_mod, scale_mod):
    floats = blended.astype(jnp.float32)
    row_mean = jnp.mean(floats, axis=-1, keepdims=True)
    centred = floats - row_mean
    row_var = jnp.mean(centred * centred, axis=-1, keepdims=True)
    return (centred * lax.rsqrt(row_var + 1e-06) * (1.0 + scale_mod) + shift_mod).astype(
        jnp.bfloat16
    )


def blend(a, wa, b, wb):
    numer = a.astype(jnp.float32) * wa + b.astype(jnp.float32) * wb
    return (numer / (wa + wb)).astype(jnp.bfloat16)


def local(latent_rows, col_weight, row_weight, shift_mod, scale_mod, w_query, w_key, w_value):
    y, x, zl, zh, c = (lax.axis_index(a) for a in AX)
    tile = y * 8 + x * 2 + zl
    gcol = tile % GC
    low = zl == 0
    top_here = (zh == 0) & (c == 0) & (tile >= GC)
    bottom_here = (zh == 3) & (c == 1) & (tile < 32 - GC)
    col_all = col_weight.astype(jnp.float32)
    row_all = row_weight.astype(jnp.float32)
    partner = jnp.where(zh == 0, jnp.maximum(tile - GC, 0), jnp.minimum(tile + GC, 31))
    left, right = latent_rows[:, :, :OV], latent_rows[:, :, OV:]
    outer = jnp.where(low, left, right)
    inner = jnp.where(low, right, left)

    def col_mix(t, v, out_other, in_other):
        own_cols = take_row(col_all, t)
        west = take_row(col_all, jnp.maximum(t - 1, 0))[OV:] * (gcol > 0)
        east = take_row(col_all, jnp.minimum(t + 1, 31))[:OV] * (gcol < GC - 1)
        other = jnp.concatenate(
            [jnp.where(low, out_other, in_other), jnp.where(low, in_other, out_other)], 2
        )
        return blend(v, own_cols[:, None], other, jnp.concatenate([west, east])[:, None])

    far_rows = lax.ppermute(latent_rows, AX, row_pairs(itself))
    far_outer = lax.ppermute(outer, AX, row_pairs(outer_of))
    far_inner = lax.ppermute(inner, AX, row_pairs(inner_of))
    out_other = lax.ppermute(outer, ("x", "zl"), OUTER_PAIRS)
    in_other = lax.ppermute(inner, "zl", SWAP)
    own = col_mix(tile, latent_rows, out_other, in_other)
    other = col_mix(partner, far_rows, far_outer, far_inner)
    own_r = lax.dynamic_slice(take_row(row_all, tile), (4 * zh + 2 * c,), (OH,))
    other_r = take_row(row_all, partner)
    other_r = jnp.where(zh == 0, other_r[14:], other_r[:OH]) * (top_here | bottom_here)
    own = blend(own, own_r[:, None, None, None], other, other_r[:, None, None, None])
    own = modulate(own, shift_mod, scale_mod).reshape(64, -1)

    def core_swap(v):
        return lax.ppermute(v, "c", SWAP)

    def weights_on(rows):
        return [
            jnp.dot(rows, w, preferred_element_type=jnp.float32).astype(jnp.bfloat16)
            for w in (w_query, w_key, w_value)
        ]

    def both_cores(v):
        return jnp.concatenate([v, core_swap(v)], 0)

    prev = lax.ppermute(own, "zh", ring(1))
    nxt = lax.ppermute(own, "zh", ring(-1))
    own_q = weights_on(own)
    prev, nxt, own_q = lax.optimization_barrier((prev, nxt, own_q))
    far = [lax.ppermute(prev[:32], "zh", ring(1)), lax.ppermute(nxt[32:], "zh", ring(-1))]
    side = jnp.concatenate([prev, nxt], 0)
    side_q = weights_on(side)
    near_x = weights_on(core_swap(jnp.concatenate([own, side], 0)))
    far, side_q, near_x = lax.optimization_barrier((far, side_q, near_x))
    far = jnp.concatenate(far, 0)
    far_q = weights_on(both_cores(far))
    at = [
        (((zh - d) % 4) * 2 + core) * 64 for core in (c, 1 - c) for d in (0, 1, 3, 2)
    ]
    return attention(jnp.stack(at).astype(jnp.int32), own_q, side_q, near_x, far_q)


def attention_kernel(at, *refs):
    parts, (out, *wholes) = refs[:12], refs[12:]

    def put(whole, n, rows):
        whole[pl.ds(pl.multiple_of(at[n], 64), 64), :] = rows

    for n, whole in enumerate(wholes):
        own, side, near_x, far = parts[n::3]
        blocks = [own[...], side[:64, :], side[64:, :], far[:64, :]]
        blocks += [near_x[m * 64 : m * 64 + 64, :] for m in range(3)] + [far[64:, :]]
        for m, rows in enumerate(blocks):
            put(whole, m, rows)
    q_all, k_all, v_all = wholes
    for h in range(out.shape[1] // HD):
        cols = slice(h * HD, h * HD + HD)
        scores = lax.dot_general(
            q_all[:, cols],
            k_all[:, cols],
            (((1,), (1,)), ((), ())),
            preferred_element_type=jnp.float32,
        ) * HD ** (-0.5)
        raised = jnp.exp(scores)
        wts = (raised / jnp.sum(raised, axis=-1, keepdims=True)).astype(jnp.bfloat16)
        out[:, cols] = jnp.dot(
            wts, v_all[:, cols], preferred_element_type=jnp.float32
        ).astype(jnp.bfloat16)


def attention(at, *groups):
    width = groups[0][0].shape[1]
    here = pl.BlockSpec(memory_space=pltpu.VMEM)
    return pl.pallas_call(
        attention_kernel,
        out_shape=jax.ShapeDtypeStruct((512, width), jnp.bfloat16),
        in_specs=[pl.BlockSpec(memory_space=pltpu.SMEM)] + [here] * 12,
        out_specs=here,
        scratch_shapes=[pltpu.VMEM((512, width), jnp.bfloat16)] * 3,
        compiler_params=pltpu.CompilerParams(vmem_limit_bytes=12 * 1024 * 1024),
    )(at, *(v for g in groups for v in g))


def solution(mesh):
    fine = Mesh(mesh.devices.reshape(4, 4, 2, 4, 2), AX)
    in_specs = (
        P(AX, None, None, None),
        P(),
        P(),
        P(),
        P(),
        P(None, ("zh", "c")),
        P(None, ("zh", "c")),
        P(None, ("zh", "c")),
    )
    out_specs = P(("y", "x", "zl"), ("zh", "c"))
    return jax.shard_map(local, mesh=fine, in_specs=in_specs, out_specs=out_specs, check_vma=False)
```

```python
import jax
import jax.numpy as jnp
from jax import lax
from jax.experimental import pallas as pl
from jax.experimental.pallas import tpu as pltpu
from jax.sharding import Mesh, PartitionSpec as P

HD = 128
GC = 4
OV = 8
OH = 2
AX = ("y", "x", "zl", "zh", "c")
SLOTS = 4


OUTER_PAIRS = [(1, 2), (2, 1), (5, 6), (6, 5)]
SWAP = [(0, 1), (1, 0)]


def ring(by):
    return [(g, (g + by) % 4) for g in range(4)]


def row_pairs(neighbour):
    pairs = []
    for t in range(32 - GC):
        n = neighbour(t)
        if n is not None:
            pairs.append((n * 8 + 7, (t + GC) * 8))
            pairs.append(((n + GC) * 8, t * 8 + 7))
    return pairs


def itself(t):
    return t


def inner_of(t):
    return t ^ 1


def outer_of(t):
    return {0: None, 1: t + 1, 2: t - 1, 3: None}[t % GC]


def take_row(table, index):
    return lax.dynamic_index_in_dim(table, index, 0, keepdims=False)


def modulate(blended, shift_mod, scale_mod):
    floats = blended.astype(jnp.float32)
    row_mean = jnp.mean(floats, axis=-1, keepdims=True)
    centred = floats - row_mean
    row_var = jnp.mean(centred * centred, axis=-1, keepdims=True)
    return (centred * lax.rsqrt(row_var + 1e-06) * (1.0 + scale_mod) + shift_mod).astype(
        jnp.bfloat16
    )


def blend(a, wa, b, wb):
    numer = a.astype(jnp.float32) * wa + b.astype(jnp.float32) * wb
    return (numer / (wa + wb)).astype(jnp.bfloat16)


def local(latent_rows, col_weight, row_weight, shift_mod, scale_mod, w_query, w_key, w_value):
    y, x, zl, zh, c = (lax.axis_index(a) for a in AX)
    tile = y * 8 + x * 2 + zl
    gcol = tile % GC
    low = zl == 0
    top_here = (zh == 0) & (c == 0) & (tile >= GC)
    bottom_here = (zh == 3) & (c == 1) & (tile < 32 - GC)
    col_all = col_weight.astype(jnp.float32)
    row_all = row_weight.astype(jnp.float32)
    partner = jnp.where(zh == 0, jnp.maximum(tile - GC, 0), jnp.minimum(tile + GC, 31))
    left, right = latent_rows[:, :, :OV], latent_rows[:, :, OV:]
    outer = jnp.where(low, left, right)
    inner = jnp.where(low, right, left)

    def col_mix(t, v, out_other, in_other):
        own_cols = take_row(col_all, t)
        west = take_row(col_all, jnp.maximum(t - 1, 0))[OV:] * (gcol > 0)
        east = take_row(col_all, jnp.minimum(t + 1, 31))[:OV] * (gcol < GC - 1)
        other = jnp.concatenate(
            [jnp.where(low, out_other, in_other), jnp.where(low, in_other, out_other)], 2
        )
        return blend(v, own_cols[:, None], other, jnp.concatenate([west, east])[:, None])

    far_rows = lax.ppermute(latent_rows, AX, row_pairs(itself))
    far_outer = lax.ppermute(outer, AX, row_pairs(outer_of))
    far_inner = lax.ppermute(inner, AX, row_pairs(inner_of))
    out_other = lax.ppermute(outer, ("x", "zl"), OUTER_PAIRS)
    in_other = lax.ppermute(inner, "zl", SWAP)
    far_rows, far_outer, far_inner, out_other, in_other = lax.optimization_barrier(
        (far_rows, far_outer, far_inner, out_other, in_other)
    )
    own = col_mix(tile, latent_rows, out_other, in_other)
    other = col_mix(partner, far_rows, far_outer, far_inner)
    own_r = lax.dynamic_slice(take_row(row_all, tile), (4 * zh + 2 * c,), (OH,))
    other_r = take_row(row_all, partner)
    other_r = jnp.where(zh == 0, other_r[14:], other_r[:OH]) * (top_here | bottom_here)
    own = blend(own, own_r[:, None, None, None], other, other_r[:, None, None, None])
    own = modulate(own, shift_mod, scale_mod).reshape(64, -1)

    def core_swap(v):
        return lax.ppermute(v, "c", SWAP)

    def weights_on(rows):
        return [
            jnp.dot(rows, w, preferred_element_type=jnp.float32).astype(jnp.bfloat16)
            for w in (w_query, w_key, w_value)
        ]

    def both_cores(v):
        return jnp.concatenate([v, core_swap(v)], 0)

    prev_a = lax.ppermute(own[:32], "zh", ring(1))
    nxt_b = lax.ppermute(own[32:], "zh", ring(-1))
    prev_b = lax.ppermute(own[32:], "zh", ring(1))
    nxt_a = lax.ppermute(own[:32], "zh", ring(-1))
    own_q = weights_on(own)
    far = [lax.ppermute(prev_a, "zh", ring(1)), lax.ppermute(nxt_b, "zh", ring(-1))]
    prev_b, nxt_a, own_q = lax.optimization_barrier((prev_b, nxt_a, own_q))
    prev, nxt = lax.optimization_barrier(
        (jnp.concatenate([prev_a, prev_b], 0), jnp.concatenate([nxt_a, nxt_b], 0))
    )
    side = jnp.concatenate([prev, nxt], 0)
    side_q = weights_on(side)
    near_x = weights_on(core_swap(jnp.concatenate([own, side], 0)))
    far, side_q, near_x = lax.optimization_barrier((far, side_q, near_x))
    far = jnp.concatenate(far, 0)
    far_q = weights_on(both_cores(far))
    at = [
        (((zh - d) % 4) * 2 + core) * 64 for core in (c, 1 - c) for d in (0, 1, 3, 2)
    ]
    return attention(jnp.stack(at).astype(jnp.int32), own_q, side_q, near_x, far_q)


def attention_kernel(at, *refs):
    parts, (out, *wholes) = refs[:12], refs[12:]

    def put(whole, n, rows):
        whole[pl.ds(pl.multiple_of(at[n], 64), 64), :] = rows

    for n, whole in enumerate(wholes):
        own, side, near_x, far = parts[n::3]
        blocks = [own[...], side[:64, :], side[64:, :], far[:64, :]]
        blocks += [near_x[m * 64 : m * 64 + 64, :] for m in range(3)] + [far[64:, :]]
        for m, rows in enumerate(blocks):
            put(whole, m, rows)
    q_all, k_all, v_all = wholes
    for h in range(out.shape[1] // HD):
        cols = slice(h * HD, h * HD + HD)
        scores = lax.dot_general(
            q_all[:, cols],
            k_all[:, cols],
            (((1,), (1,)), ((), ())),
            preferred_element_type=jnp.float32,
        ) * HD ** (-0.5)
        raised = jnp.exp(scores)
        wts = (raised / jnp.sum(raised, axis=-1, keepdims=True)).astype(jnp.bfloat16)
        out[:, cols] = jnp.dot(
            wts, v_all[:, cols], preferred_element_type=jnp.float32
        ).astype(jnp.bfloat16)


def attention(at, *groups):
    width = groups[0][0].shape[1]
    here = pl.BlockSpec(memory_space=pltpu.VMEM)
    return pl.pallas_call(
        attention_kernel,
        out_shape=jax.ShapeDtypeStruct((512, width), jnp.bfloat16),
        in_specs=[pl.BlockSpec(memory_space=pltpu.SMEM)] + [here] * 12,
        out_specs=here,
        scratch_shapes=[pltpu.VMEM((512, width), jnp.bfloat16)] * 3,
        compiler_params=pltpu.CompilerParams(vmem_limit_bytes=12 * 1024 * 1024),
    )(at, *(v for g in groups for v in g))


def solution(mesh):
    fine = Mesh(mesh.devices.reshape(4, 4, 2, 4, 2), AX)
    in_specs = (
        P(AX, None, None, None),
        P(),
        P(),
        P(),
        P(),
        P(None, ("zh", "c")),
        P(None, ("zh", "c")),
        P(None, ("zh", "c")),
    )
    out_specs = P(("y", "x", "zl"), ("zh", "c"))
    return jax.shard_map(local, mesh=fine, in_specs=in_specs, out_specs=out_specs, check_vma=False)
```

```python
import jax
import jax.numpy as jnp
from jax import lax
from jax.experimental import pallas as pl
from jax.experimental.pallas import tpu as pltpu
from jax.sharding import Mesh, PartitionSpec as P

HD = 128
GC = 4
OV = 8
OH = 2
AX = ("y", "x", "zl", "zh", "c")
SLOTS = 4


OUTER_PAIRS = [(1, 2), (2, 1), (5, 6), (6, 5)]
SWAP = [(0, 1), (1, 0)]


def ring(by):
    return [
        (g * 2 + c, ((g + (by if c == 0 else -by)) % 4) * 2 + c) for g in range(4) for c in range(2)
    ]


def row_pairs(neighbour):
    pairs = []
    for t in range(32 - GC):
        n = neighbour(t)
        if n is not None:
            pairs.append((n * 8 + 7, (t + GC) * 8))
            pairs.append(((n + GC) * 8, t * 8 + 7))
    return pairs


def itself(t):
    return t


def inner_of(t):
    return t ^ 1


def outer_of(t):
    return {0: None, 1: t + 1, 2: t - 1, 3: None}[t % GC]


def take_row(table, index):
    return lax.dynamic_index_in_dim(table, index, 0, keepdims=False)


def modulate(blended, shift_mod, scale_mod):
    floats = blended.astype(jnp.float32)
    row_mean = jnp.mean(floats, axis=-1, keepdims=True)
    centred = floats - row_mean
    row_var = jnp.mean(centred * centred, axis=-1, keepdims=True)
    return (centred * lax.rsqrt(row_var + 1e-06) * (1.0 + scale_mod) + shift_mod).astype(
        jnp.bfloat16
    )


def blend(a, wa, b, wb):
    numer = a.astype(jnp.float32) * wa + b.astype(jnp.float32) * wb
    return (numer / (wa + wb)).astype(jnp.bfloat16)


def local(latent_rows, col_weight, row_weight, shift_mod, scale_mod, w_query, w_key, w_value):
    y, x, zl, zh, c = (lax.axis_index(a) for a in AX)
    tile = y * 8 + x * 2 + zl
    gcol = tile % GC
    low = zl == 0
    top_here = (zh == 0) & (c == 0) & (tile >= GC)
    bottom_here = (zh == 3) & (c == 1) & (tile < 32 - GC)
    col_all = col_weight.astype(jnp.float32)
    row_all = row_weight.astype(jnp.float32)
    partner = jnp.where(zh == 0, jnp.maximum(tile - GC, 0), jnp.minimum(tile + GC, 31))
    left, right = latent_rows[:, :, :OV], latent_rows[:, :, OV:]
    outer = jnp.where(low, left, right)
    inner = jnp.where(low, right, left)

    def col_mix(t, v, out_other, in_other):
        own_cols = take_row(col_all, t)
        west = take_row(col_all, jnp.maximum(t - 1, 0))[OV:] * (gcol > 0)
        east = take_row(col_all, jnp.minimum(t + 1, 31))[:OV] * (gcol < GC - 1)
        other = jnp.concatenate(
            [jnp.where(low, out_other, in_other), jnp.where(low, in_other, out_other)], 2
        )
        return blend(v, own_cols[:, None], other, jnp.concatenate([west, east])[:, None])

    far_rows = lax.ppermute(latent_rows, AX, row_pairs(itself))
    far_outer = lax.ppermute(outer, AX, row_pairs(outer_of))
    far_inner = lax.ppermute(inner, AX, row_pairs(inner_of))
    out_other = lax.ppermute(outer, ("x", "zl"), OUTER_PAIRS)
    in_other = lax.ppermute(inner, "zl", SWAP)
    far_rows, far_outer, far_inner, out_other, in_other = lax.optimization_barrier(
        (far_rows, far_outer, far_inner, out_other, in_other)
    )
    own = col_mix(tile, latent_rows, out_other, in_other)
    other = col_mix(partner, far_rows, far_outer, far_inner)
    own_r = lax.dynamic_slice(take_row(row_all, tile), (4 * zh + 2 * c,), (OH,))
    other_r = take_row(row_all, partner)
    other_r = jnp.where(zh == 0, other_r[14:], other_r[:OH]) * (top_here | bottom_here)
    own = blend(own, own_r[:, None, None, None], other, other_r[:, None, None, None])
    own = modulate(own, shift_mod, scale_mod).reshape(64, -1)

    def core_swap(v):
        return lax.ppermute(v, "c", SWAP)

    def weights_on(rows):
        return [
            jnp.dot(rows, w, preferred_element_type=jnp.float32).astype(jnp.bfloat16)
            for w in (w_query, w_key, w_value)
        ]

    def both_cores(v):
        return jnp.concatenate([v, core_swap(v)], 0)

    prev_a = lax.ppermute(own[:32], ("zh", "c"), ring(1))
    nxt_b = lax.ppermute(own[32:], ("zh", "c"), ring(-1))
    prev_b = lax.ppermute(own[32:], ("zh", "c"), ring(1))
    nxt_a = lax.ppermute(own[:32], ("zh", "c"), ring(-1))
    own_q = weights_on(own)
    far = [lax.ppermute(prev_a, ("zh", "c"), ring(1)), lax.ppermute(nxt_b, ("zh", "c"), ring(-1))]
    prev_b, nxt_a, own_q = lax.optimization_barrier((prev_b, nxt_a, own_q))
    prev, nxt = lax.optimization_barrier(
        (jnp.concatenate([prev_a, prev_b], 0), jnp.concatenate([nxt_a, nxt_b], 0))
    )
    side = jnp.concatenate([prev, nxt], 0)
    side_q = weights_on(side)
    near_x = weights_on(core_swap(jnp.concatenate([own, side], 0)))
    far, side_q, near_x = lax.optimization_barrier((far, side_q, near_x))
    far = jnp.concatenate(far, 0)
    far_q = weights_on(both_cores(far))
    at = [
        (((zh - d) % 4) * 2 + core) * 64 for core in (c, 1 - c) for d in (0, 1 + 2 * core, 3 - 2 * core, 2)
    ]
    return attention(jnp.stack(at).astype(jnp.int32), own_q, side_q, near_x, far_q)


def attention_kernel(at, *refs):
    parts, (out, *wholes) = refs[:12], refs[12:]

    def put(whole, n, rows):
        whole[pl.ds(pl.multiple_of(at[n], 64), 64), :] = rows

    for n, whole in enumerate(wholes):
        own, side, near_x, far = parts[n::3]
        blocks = [own[...], side[:64, :], side[64:, :], far[:64, :]]
        blocks += [near_x[m * 64 : m * 64 + 64, :] for m in range(3)] + [far[64:, :]]
        for m, rows in enumerate(blocks):
            put(whole, m, rows)
    q_all, k_all, v_all = wholes
    for h in range(out.shape[1] // HD):
        cols = slice(h * HD, h * HD + HD)
        scores = lax.dot_general(
            q_all[:, cols],
            k_all[:, cols],
            (((1,), (1,)), ((), ())),
            preferred_element_type=jnp.float32,
        ) * HD ** (-0.5)
        raised = jnp.exp(scores)
        wts = (raised / jnp.sum(raised, axis=-1, keepdims=True)).astype(jnp.bfloat16)
        out[:, cols] = jnp.dot(
            wts, v_all[:, cols], preferred_element_type=jnp.float32
        ).astype(jnp.bfloat16)


def attention(at, *groups):
    width = groups[0][0].shape[1]
    here = pl.BlockSpec(memory_space=pltpu.VMEM)
    return pl.pallas_call(
        attention_kernel,
        out_shape=jax.ShapeDtypeStruct((512, width), jnp.bfloat16),
        in_specs=[pl.BlockSpec(memory_space=pltpu.SMEM)] + [here] * 12,
        out_specs=here,
        scratch_shapes=[pltpu.VMEM((512, width), jnp.bfloat16)] * 3,
        compiler_params=pltpu.CompilerParams(vmem_limit_bytes=12 * 1024 * 1024),
    )(at, *(v for g in groups for v in g))


def solution(mesh):
    fine = Mesh(mesh.devices.reshape(4, 4, 2, 4, 2), AX)
    in_specs = (
        P(AX, None, None, None),
        P(),
        P(),
        P(),
        P(),
        P(None, ("zh", "c")),
        P(None, ("zh", "c")),
        P(None, ("zh", "c")),
    )
    out_specs = P(("y", "x", "zl"), ("zh", "c"))
    return jax.shard_map(local, mesh=fine, in_specs=in_specs, out_specs=out_specs, check_vma=False)
```
